32 devices in a mesh: rows: 16 (over z, y, core), grp: 2 (over x).
Axes of the slice: x: 2, y: 2, z: 4, core: 2. Of those that a mesh axis runs over, the one named last changes fastest.
Arguments:
- a_tiles: bfloat16 [512, 64, 1728], P(('rows', 'grp')), may hold values from -0.15625 to 0.15625
- p_tiles: bfloat16 [512, 64, 192], P(('rows', 'grp')), may hold values from -0.75 to 0.75
- acols: int32 [512, 27], P(('rows', 'grp')), may hold values from 0 to 511, as said below
- agg: int32 [512], replicated, may hold values from 0 to 63, as said below
Outputs:
- coarse_op: float32 [64, 64, 704], P(('rows', 'grp'))
The draws below stay inside these ranges and needn't reach their ends.
Inputs may be any that keep to these rules, and one draw needn't show every extreme that they name: `acols`: the 27 block columns of row i are distinct, each (i + o) mod 512 with o in -14..14; o = 0, -14 and 14 are always among them. agg never falls; aggregate c begins at fine block row 8 * c + r_c with r_c = 0 for even c and |r_c| at most 4 for odd c, so every aggregate has 4 to 12 rows, and some aggregate has 12.
All inputs are finite; a program needn't handle non-finite values.
Results may differ from the reference program's by a relative error of at most 0.0029.
Values may be sent and summed in bfloat16 or wider, within the bound.
A program may use at most 64 MiB of HBM per device.

```python
import jax
import jax.numpy as jnp
from jax import lax

TILE = 64
KA = 27
PCOLS = 3
RATIO = 8
REACH = 14
NB = 512
NC = 64


def draw_acols(key, part):
    rows_all = jnp.arange(NB, dtype=jnp.int32)
    candidates = jnp.concatenate([jnp.arange(-REACH + 1, 0, dtype=jnp.int32), jnp.arange(1, REACH, dtype=jnp.int32)])
    width_count = 2 * REACH - 2
    scores = jax.random.randint(key, (NB, width_count), 0, 1 << 20) * (2 * REACH) + jnp.arange(width_count, dtype=jnp.int32)[None, :]
    order = jnp.argsort(scores, axis=1, stable=True)
    picked = jnp.take(candidates, order[:, :KA - 3])
    fixed_part = jnp.broadcast_to(jnp.array([0, -REACH, REACH], dtype=jnp.int32)[None, :], (NB, 3))
    offsets = jnp.concatenate([fixed_part, picked], axis=1)
    return ((rows_all[:, None] + offsets) % NB).astype(jnp.int32)


def draw_agg(key, part):
    half_count = NC // 2
    spread = jax.random.randint(key, (half_count,), -(RATIO // 2), RATIO // 2 + 1).astype(jnp.int32)
    spread = spread.at[0].set(RATIO // 2)
    lengths = jnp.stack([RATIO + spread, RATIO - spread], axis=1).reshape(NC)
    starts = jnp.cumsum(lengths) - lengths
    marks = jnp.zeros((NB,), jnp.int32).at[starts[1:]].add(1)
    return jnp.cumsum(marks).astype(jnp.int32)


def level_of(own_key, extent, shards, smallest, top_value):
    def one(axis_at, blocks):
        steps = jax.random.uniform(jax.random.fold_in(jax.random.fold_in(own_key, 6), axis_at), (blocks,), jnp.float32, smallest / len(shards), top_value / len(shards))
        return jnp.repeat(jnp.exp(steps), extent[axis_at] // blocks).reshape((-1,) + (1,) * (len(extent) - axis_at - 1))

    factor_of = one(*shards[0])
    for cut in shards[1:]:
        factor_of = factor_of * one(*cut)
    return factor_of


def scatter_about(rng, extent, scale, limit, cuts=(), kind=jnp.bfloat16):
    drawn = jax.random.normal(rng, extent, jnp.float32) * scale
    if len(cuts) > 0:
        drawn = level_of(rng, extent, cuts, -0.22, 0.18) * drawn
    return jnp.clip(drawn, min=-limit, max=limit).astype(kind)


def setup_inputs(seed: int = 0) -> dict:
    splits = jax.random.split(jax.random.key(seed), 5)
    return {
        "a_tiles": scatter_about(splits[0], (NB, TILE, KA * TILE), (KA * TILE) ** -0.5, 0.15625, ((0, 32),)),
        "p_tiles": scatter_about(splits[1], (NB, TILE, PCOLS * TILE), TILE ** -0.5, 0.75, ((0, 32),)),
        "acols": draw_acols(jax.random.fold_in(splits[4], 71), 0),
        "agg": draw_agg(jax.random.fold_in(splits[4], 71), 0),
    }


def tile_bands(a_block, p_pick, shifts):
    row_count = a_block.shape[0]
    tile_size = a_block.shape[1]
    link_count = p_pick.shape[1]
    blocks = a_block.reshape(row_count, tile_size, link_count, tile_size).astype(jnp.float32)
    products = jnp.einsum('brkc,bkcq->bkrq', blocks, p_pick.astype(jnp.float32), precision=lax.Precision.HIGHEST)
    onehot = (shifts[:, :, None] == jnp.arange(7, dtype=jnp.int32)[None, None, :]).astype(jnp.float32)
    grouped = jnp.einsum('bks,bkrq->bsrq', onehot, products, precision=lax.Precision.HIGHEST)
    widened = jnp.zeros((row_count, tile_size, 9 * tile_size), jnp.float32)
    for offset in range(7):
        widened = widened + jnp.pad(grouped[:, offset], ((0, 0), (0, 0), (offset * tile_size, (6 - offset) * tile_size)))
    return widened.astype(jnp.bfloat16)


def reference(a_tiles, p_tiles, acols, agg):
    block_rows = 64
    def one_block(accumulated, block_index):
        row_start = block_index * block_rows
        a_block = lax.dynamic_slice_in_dim(a_tiles, row_start, block_rows, 0)
        p_block = lax.dynamic_slice_in_dim(p_tiles, row_start, block_rows, 0)
        own_cols = lax.dynamic_slice_in_dim(acols, row_start, block_rows, 0)
        own_agg = lax.dynamic_slice_in_dim(agg, row_start, block_rows, 0)
        p_pick = jnp.take(p_tiles, own_cols, axis=0)
        shifts = ((jnp.take(agg, own_cols) - own_agg[:, None] + 3) % NC).astype(jnp.int32)
        widened = tile_bands(a_block, p_pick, shifts).astype(jnp.float32)
        for column in range(PCOLS):
            p_column = p_block[:, :, column * TILE:(column + 1) * TILE].astype(jnp.float32)
            coarse_term = jnp.einsum('brc,brq->bcq', p_column, widened, precision=lax.Precision.HIGHEST)
            coarse_term = jnp.pad(coarse_term, ((0, 0), (0, 0), ((2 - column) * TILE, column * TILE)))
            target = ((own_agg + column - 1) % NC).astype(jnp.int32)
            accumulated = accumulated.at[target].add(coarse_term)
        return accumulated, None
    initial = jnp.zeros((NC, TILE, 11 * TILE), jnp.float32)
    coarse_op, _ = lax.scan(one_block, initial, jnp.arange(NB // block_rows, dtype=jnp.int32))
    return coarse_op
```

```python
import functools

import jax
import jax.numpy as jnp
from jax import lax
from jax.experimental import pallas as pl
from jax.experimental.pallas import tpu as pltpu
from jax.sharding import PartitionSpec as P

RATIO = 8
REACH = 14
MESH = pl.DeviceIdType.MESH


def dot(a, b):
    return jnp.dot(a, b, preferred_element_type=jnp.float32)


def galerkin_kernel(
    rows_dev, tile, links, ring, grp, agg, acols, a_hbm, p_hbm, out,
    found, tbl, a2, a_tail, p_own, p_left, p_right, ad, p4, p4t, band, part, got_left, got_right,
    a_sem, p_sem, t_sem, halo_send, halo_recv, part_send, part_recv,
):
    lane = 2 * tile
    halo = REACH
    pairs = (links + 1) // 2
    groups = rows_dev // 2 + halo
    me = lax.axis_index("rows") * grp + lax.axis_index("grp")
    right, left = lax.rem(me + 1, ring), lax.rem(me + ring - 1, ring)

    def device(d):
        return (d // grp, lax.rem(d, grp))

    full = links // 2
    a_copies = [
        pltpu.make_async_copy(
            a_hbm.at[:, :, pl.ds(g * lane, lane)], a2.at[g], a_sem.at[g]
        )
        for g in range(full)
    ]
    a_copies.append(
        pltpu.make_async_copy(
            a_hbm.at[:, :, pl.ds(full * lane, tile)], a_tail, a_sem.at[full]
        )
    )
    p_copy = pltpu.make_async_copy(p_hbm, p_own, p_sem)
    p_copy.start()
    for copy in a_copies:
        copy.start()

    barrier = pltpu.get_barrier_semaphore()
    for neighbour in (left, right):
        pl.semaphore_signal(barrier, inc=1, device_id=device(neighbour), device_id_type=MESH)
    pl.semaphore_wait(barrier, 2)

    to_right = pltpu.make_async_remote_copy(
        p_hbm.at[pl.ds(rows_dev - halo, halo)], p_left,
        halo_send.at[0], halo_recv.at[0], device_id=device(right), device_id_type=MESH,
    )
    to_left = pltpu.make_async_remote_copy(
        p_hbm.at[pl.ds(0, halo)], p_right,
        halo_send.at[1], halo_recv.at[1], device_id=device(left), device_id_type=MESH,
    )
    to_right.start()
    to_left.start()

    total_rows = rows_dev * ring
    first_row = me * rows_dev
    row = lax.broadcasted_iota(jnp.int32, found.shape, 0)
    spot = lax.broadcasted_iota(jnp.int32, found.shape, 1)
    half = spot & 1
    table = (half if links % 2 == 0 else 1 - half) * pairs + links // 2
    for k in range(links):
        at = jnp.broadcast_to(acols[:, k : k + 1], found.shape) - first_row - row + REACH
        at = jnp.where(at < 0, at + total_rows, at)
        at = jnp.where(at >= total_rows, at - total_rows, at) + (row & 1)
        side = half if k % 2 == 0 else 1 - half
        table = jnp.where(at == spot, side * pairs + k // 2, table)
    found[...] = table
    t_copy = pltpu.make_async_copy(found, tbl, t_sem)
    t_copy.start()

    def place(p_ref, count, base):
        def step(r, carry):
            x = p_ref[r]
            own = agg[lax.rem(first_row + total_rows - halo + base + r, total_rows)] & 1
            odd = jnp.full((tile, 4 * tile), own, jnp.int32).astype(jnp.float32).astype(jnp.bfloat16)
            gap = jnp.zeros((tile, tile), jnp.bfloat16)
            low = jnp.concatenate([x, gap], axis=1)
            high = jnp.concatenate([gap, x], axis=1)
            p4[pl.ds(pl.multiple_of((base + r) * tile, tile), tile), :] = (
                low * (jnp.bfloat16(1) - odd) + high * odd
            )
            return carry

        lax.fori_loop(0, count, step, 0)

    p_copy.wait()
    place(p_own, rows_dev, halo)
    p4t[...] = p4[halo * tile : (halo + rows_dev) * tile, :].T

    def swap(g):
        def step(r, carry):
            x = a2[g, r]
            a2[pairs + g, r] = jnp.concatenate([x[:, tile:], x[:, :tile]], axis=1)
            return carry

        lax.fori_loop(0, rows_dev, step, 0)

    for g in range(full):
        a_copies[g].wait()
        swap(g)
    a_copies[full].wait()

    def swap_tail(r, carry):
        x, gap = a_tail[r], jnp.zeros((tile, tile), jnp.bfloat16)
        a2[full, r] = jnp.concatenate([x, gap], axis=1)
        a2[pairs + full, r] = jnp.concatenate([gap, x], axis=1)
        return carry

    lax.fori_loop(0, rows_dev, swap_tail, 0)
    t_copy.wait()

    span = REACH + 1
    first_half = lax.broadcasted_iota(jnp.int32, (tile, lane), 1) < tile

    def gather(r2, carry):
        for parity in range(2):
            r = 2 * r2 + parity
            rows = pl.ds(pl.multiple_of(r * tile, tile), tile)
            for g in range(span):
                x0 = a2[tbl[r, 2 * g], r]
                x1 = a2[tbl[r, 2 * g + 1], r]
                ad[rows, pl.ds(pl.multiple_of((r2 + g) * lane, lane), lane)] = jnp.where(
                    first_half, x0, x1
                )
        return carry

    lax.fori_loop(0, rows_dev // 2, gather, 0)

    empty = jnp.zeros((2 * tile, lane), jnp.bfloat16)
    for r2 in range(rows_dev // 2):
        for g in range(groups):
            if g < r2 or g >= r2 + span:
                ad[r2 * lane : (r2 + 1) * lane, g * lane : (g + 1) * lane] = empty

    chunk = 4 * tile
    k_left, k_own, k_all = halo * tile, (halo + rows_dev) * tile, (2 * halo + rows_dev) * tile
    own_sum = part

    def own_part(c, carry):
        rows = pl.ds(pl.multiple_of(c * chunk, chunk), chunk)
        own_sum[rows, :] = dot(ad[rows, k_left:k_own], p4[k_left:k_own, :])
        return carry

    lax.fori_loop(0, rows_dev // 4, own_part, 0)

    to_right.wait()
    place(p_left, halo, 0)
    to_left.wait()
    place(p_right, halo, halo + rows_dev)

    def ends(c, carry):
        rows = pl.ds(pl.multiple_of(c * chunk, chunk), chunk)
        low = dot(ad[rows, 0:k_left], p4[0:k_left, :])
        high = dot(ad[rows, k_own:k_all], p4[k_own:k_all, :])
        mid = own_sum[rows, :]
        band[rows, 0:lane] = low[:, :lane].astype(jnp.bfloat16)
        band[rows, lane : 2 * lane] = (low[:, lane:] + mid[:, :lane]).astype(jnp.bfloat16)
        band[rows, 2 * lane : 3 * lane] = (high[:, :lane] + mid[:, lane:]).astype(jnp.bfloat16)
        band[rows, 3 * lane : 4 * lane] = high[:, lane:].astype(jnp.bfloat16)
        return carry

    lax.fori_loop(0, rows_dev // 4, ends, 0)

    send_left, send_right = got_left.at[1], got_right.at[1]
    outer = dot(p4t[0:tile, :], band[...])
    send_left[...] = outer.astype(jnp.bfloat16)
    part_left = pltpu.make_async_remote_copy(
        send_left, got_right.at[0],
        part_send.at[0], part_recv.at[0], device_id=device(left), device_id_type=MESH,
    )
    part_left.start()
    outer = dot(p4t[3 * tile : 4 * tile, :], band[...])
    send_right[...] = outer.astype(jnp.bfloat16)
    part_right = pltpu.make_async_remote_copy(
        send_right, got_left.at[0],
        part_send.at[1], part_recv.at[1], device_id=device(right), device_id_type=MESH,
    )
    part_right.start()
    inner = dot(p4t[tile : 3 * tile, :], band[...])
    even, odd = inner[:tile], inner[tile:]

    edge = jnp.zeros((tile, lane), jnp.float32)
    even = jnp.concatenate([edge, even, jnp.zeros((tile, tile), jnp.float32)], axis=1)
    part_right.wait()
    from_left = got_left[0].astype(jnp.float32)
    out[0] = even + jnp.concatenate([from_left, jnp.zeros((tile, 3 * tile), jnp.float32)], axis=1)
    part_left.wait()
    from_right = got_right[0].astype(jnp.float32)
    odd = jnp.concatenate([odd, edge], axis=1) + jnp.concatenate([edge, from_right], axis=1)
    out[1] = jnp.concatenate([jnp.zeros((tile, tile), jnp.float32), odd], axis=1)


def shards(a_tiles, p_tiles, acols, agg):
    rows_dev, tile, width = a_tiles.shape
    links = width // tile
    grp = lax.axis_size("grp")
    ring = lax.axis_size("rows") * grp
    halo = REACH
    bf16, f32 = jnp.bfloat16, jnp.float32
    pairs = (links + 1) // 2
    lane = 2 * tile
    n_all = rows_dev + 2 * halo
    return pl.pallas_call(
        functools.partial(galerkin_kernel, rows_dev, tile, links, ring, grp),
        out_shape=jax.ShapeDtypeStruct((rows_dev // RATIO, tile, 11 * tile), f32),
        in_specs=[
            pl.BlockSpec(memory_space=pltpu.SMEM),
            pl.BlockSpec(memory_space=pltpu.VMEM),
            pl.BlockSpec(memory_space=pl.ANY),
            pl.BlockSpec(memory_space=pl.ANY),
        ],
        out_specs=pl.BlockSpec(memory_space=pltpu.VMEM),
        scratch_shapes=[
            pltpu.VMEM((rows_dev, lane), jnp.int32),
            pltpu.SMEM((rows_dev, lane), jnp.int32),
            pltpu.VMEM((2 * pairs, rows_dev, tile, lane), bf16),
            pltpu.VMEM((rows_dev, tile, tile), bf16),
            pltpu.VMEM((rows_dev, tile, 3 * tile), bf16),
            pltpu.VMEM((halo, tile, 3 * tile), bf16),
            pltpu.VMEM((halo, tile, 3 * tile), bf16),
            pltpu.VMEM((rows_dev * tile, n_all * tile), bf16),
            pltpu.VMEM((n_all * tile, 4 * tile), bf16),
            pltpu.VMEM((4 * tile, rows_dev * tile), bf16),
            pltpu.VMEM((rows_dev * tile, 8 * tile), bf16),
            pltpu.VMEM((rows_dev * tile, 4 * tile), f32),
            pltpu.VMEM((2, tile, 8 * tile), bf16),
            pltpu.VMEM((2, tile, 8 * tile), bf16),
            pltpu.SemaphoreType.DMA((pairs,)),
            pltpu.SemaphoreType.DMA,
            pltpu.SemaphoreType.DMA,
            pltpu.SemaphoreType.DMA((2,)),
            pltpu.SemaphoreType.DMA((2,)),
            pltpu.SemaphoreType.DMA((2,)),
            pltpu.SemaphoreType.DMA((2,)),
        ],
        compiler_params=pltpu.CompilerParams(
            collective_id=0, has_side_effects=True, vmem_limit_bytes=60 * 2**20
        ),
    )(agg, acols, a_tiles, p_tiles)


def solution(mesh):
    return jax.shard_map(
        shards,
        mesh=mesh,
        in_specs=(
            P(("rows", "grp"), None, None),
            P(("rows", "grp"), None, None),
            P(("rows", "grp"), None),
            P(),
        ),
        out_specs=P(("rows", "grp"), None, None),
        check_vma=False,
    )
```

```python
import functools

import jax
import jax.numpy as jnp
from jax import lax
from jax.experimental import pallas as pl
from jax.experimental.pallas import tpu as pltpu
from jax.sharding import PartitionSpec as P

RATIO = 8
REACH = 14
MESH = pl.DeviceIdType.MESH


def dot(a, b):
    return jnp.dot(a, b, preferred_element_type=jnp.float32)


def galerkin_kernel(
    rows_dev, tile, links, ring, grp, agg, acols, a_hbm, p_hbm, out,
    found, tbl, a2, a_tail, p_own, packed, near, ad, p4, p4t, band, part, got_left, got_right,
    a_sem, p_sem, t_sem, halo_send, halo_recv, part_send, part_recv,
):
    lane = 2 * tile
    halo = REACH
    pairs = (links + 1) // 2
    groups = rows_dev // 2 + halo
    me = lax.axis_index("rows") * grp + lax.axis_index("grp")
    right, left = lax.rem(me + 1, ring), lax.rem(me + ring - 1, ring)

    def device(d):
        return (d // grp, lax.rem(d, grp))

    full = links // 2
    a_copies = [
        pltpu.make_async_copy(
            a_hbm.at[:, :, pl.ds(g * lane, lane)], a2.at[g], a_sem.at[g]
        )
        for g in range(full)
    ]
    a_copies.append(
        pltpu.make_async_copy(
            a_hbm.at[:, :, pl.ds(full * lane, tile)], a_tail, a_sem.at[full]
        )
    )
    p_copy = pltpu.make_async_copy(p_hbm, p_own, p_sem)
    p_copy.start()
    for copy in a_copies:
        copy.start()

    barrier = pltpu.get_barrier_semaphore()
    for step in (1, 2, ring - 2, ring - 1):
        pl.semaphore_signal(
            barrier, inc=1, device_id=device(lax.rem(me + step, ring)), device_id_type=MESH
        )

    p_copy.wait()
    for r in range(rows_dev):
        x = p_own[r]
        packed[r, :tile] = x[:, :lane]
        packed[r, tile:] = jnp.concatenate([x[: tile // 2, lane:], x[tile // 2 :, lane:]], axis=1)
    pl.semaphore_wait(barrier, 4)

    spot4 = lax.rem(me, 4)
    core = spot4 // 2
    is_inner = (spot4 == 1) | (spot4 == 2)
    is_outer = (spot4 == 0) | (spot4 == 3)
    mate = lax.rem(me + 2 + ring - 4 * core, ring)
    mid, spare = rows_dev // 2, rows_dev - halo

    def send(src, side, start, count, sem, arrival, target):
        return pltpu.make_async_remote_copy(
            src.at[pl.ds(start, count)], near.at[side, pl.ds(start, count)],
            halo_send.at[sem], halo_recv.at[arrival],
            device_id=device(target), device_id_type=MESH,
        )

    to_right = send(packed, 0, spare, halo, 0, 2, right)
    to_left = send(packed, 1, 0, halo, 1, 2, left)
    half_low = send(packed, 1, 0, mid, 0, 0, left)
    half_high = send(packed, 0, mid, mid, 1, 0, right)
    got_half = near.at[1 - core]
    swap_half = send(got_half, core, mid * core, mid, 2, 1, mate)
    in_half = send(packed, 1 - core, mid * core, mid, 2, 0, mate)
    in_swap = send(packed, 1 - core, mid * (1 - core), mid, 2, 1, mate)
    in_full = send(packed, core, spare * (1 - core), halo, 2, 2, mate)

    @pl.when(is_inner)
    def _():
        half_low.start()
        half_high.start()

    @pl.when(is_outer)
    def _():
        to_right.start()
        to_left.start()

    total_rows = rows_dev * ring
    first_row = me * rows_dev
    row = lax.broadcasted_iota(jnp.int32, found.shape, 0)
    spot = lax.broadcasted_iota(jnp.int32, found.shape, 1)
    half = spot & 1
    table = (half if links % 2 == 0 else 1 - half) * pairs + links // 2
    for k in range(links):
        at = jnp.broadcast_to(acols[:, k : k + 1], found.shape) - first_row - row + REACH
        at = jnp.where(at < 0, at + total_rows, at)
        at = jnp.where(at >= total_rows, at - total_rows, at) + (row & 1)
        side = half if k % 2 == 0 else 1 - half
        table = jnp.where(at == spot, side * pairs + k // 2, table)
    found[...] = table
    t_copy = pltpu.make_async_copy(found, tbl, t_sem)
    t_copy.start()

    low_half = lax.broadcasted_iota(jnp.int32, (tile, lane), 1) < tile

    def place(p_ref, from_row, count, base):
        nothing = jnp.zeros((tile, lane), jnp.bfloat16)
        for r in range(count):
            x, y = p_ref[from_row + r, :tile], p_ref[from_row + r, tile:]
            turned = pltpu.roll(y, tile, 1)
            rest_low = jnp.concatenate([y, turned], axis=0)
            rest_high = jnp.concatenate([turned, y], axis=0)
            x_turned = pltpu.roll(x, tile, 1)
            own = agg[lax.rem(first_row + total_rows - halo + base + r, total_rows)] & 1
            odd = jnp.full((tile, lane), own, jnp.int32).astype(jnp.float32).astype(jnp.bfloat16)
            even = jnp.bfloat16(1) - odd
            rows = slice((base + r) * tile, (base + r + 1) * tile)
            p4[rows, :lane] = x * even + jnp.where(low_half, nothing, x_turned) * odd
            p4[rows, lane:] = (
                jnp.where(low_half, rest_low, nothing) * even
                + jnp.where(low_half, x_turned, rest_high) * odd
            )

    place(packed, 0, rows_dev, halo)
    p4t[...] = p4[halo * tile : (halo + rows_dev) * tile, :].T

    for copy in a_copies:
        copy.wait()
    gap = jnp.zeros((tile, tile), jnp.bfloat16)
    for r in range(rows_dev):
        x = a_tail[r]
        a2[full, r] = jnp.concatenate([x, gap], axis=1)
        a2[pairs + full, r] = jnp.concatenate([gap, x], axis=1)

    def swap(g, carry):
        for r in range(rows_dev):
            a2[pairs + g, r] = pltpu.roll(a2[g, r], tile, 1)
        return carry

    lax.fori_loop(0, full, swap, 0)
    t_copy.wait()

    span = REACH + 1
    first_half = lax.broadcasted_iota(jnp.int32, (tile, lane), 1) < tile

    def gather(r2, carry):
        for parity in range(2):
            r = 2 * r2 + parity
            rows = pl.ds(pl.multiple_of(r * tile, tile), tile)
            for g in range(span):
                x0 = a2[tbl[r, 2 * g], r]
                x1 = a2[tbl[r, 2 * g + 1], r]
                ad[rows, pl.ds(pl.multiple_of((r2 + g) * lane, lane), lane)] = jnp.where(
                    first_half, x0, x1
                )
        return carry

    lax.fori_loop(0, rows_dev // 2, gather, 0)

    empty = jnp.zeros((2 * tile, lane), jnp.bfloat16)
    for r2 in range(rows_dev // 2):
        for g in range(groups):
            if g < r2 or g >= r2 + span:
                ad[r2 * lane : (r2 + 1) * lane, g * lane : (g + 1) * lane] = empty

    chunk = 4 * tile
    k_left, k_own, k_all = halo * tile, (halo + rows_dev) * tile, (2 * halo + rows_dev) * tile
    own_sum = part

    def own_part(c, carry):
        rows = pl.ds(pl.multiple_of(c * chunk, chunk), chunk)
        own_sum[rows, :] = dot(ad[rows, k_left:k_own], p4[k_left:k_own, :])
        return carry

    lax.fori_loop(0, rows_dev // 4, own_part, 0)

    in_half.wait_recv()
    swap_half.start()
    in_full.wait_recv()
    in_swap.wait_recv()
    place(near.at[0], spare, halo, 0)
    place(near.at[1], 0, halo, halo + rows_dev)

    def ends(c, carry):
        rows = pl.ds(pl.multiple_of(c * chunk, chunk), chunk)
        low = dot(ad[rows, 0:k_left], p4[0:k_left, :])
        high = dot(ad[rows, k_own:k_all], p4[k_own:k_all, :])
        mid = own_sum[rows, :]
        band[rows, 0:lane] = low[:, :lane].astype(jnp.bfloat16)
        band[rows, lane : 2 * lane] = (low[:, lane:] + mid[:, :lane]).astype(jnp.bfloat16)
        band[rows, 2 * lane : 3 * lane] = (high[:, :lane] + mid[:, lane:]).astype(jnp.bfloat16)
        band[rows, 3 * lane : 4 * lane] = high[:, lane:].astype(jnp.bfloat16)
        return carry

    lax.fori_loop(0, rows_dev // 4, ends, 0)

    send_left, send_right = got_left.at[1], got_right.at[1]
    outer = dot(p4t[0:tile, :], band[...])
    send_left[...] = outer.astype(jnp.bfloat16)
    part_left = pltpu.make_async_remote_copy(
        send_left, got_right.at[0],
        part_send.at[0], part_recv.at[0], device_id=device(left), device_id_type=MESH,
    )
    part_left.start()
    outer = dot(p4t[3 * tile : 4 * tile, :], band[...])
    send_right[...] = outer.astype(jnp.bfloat16)
    part_right = pltpu.make_async_remote_copy(
        send_right, got_left.at[0],
        part_send.at[1], part_recv.at[1], device_id=device(right), device_id_type=MESH,
    )
    part_right.start()
    inner = dot(p4t[tile : 3 * tile, :], band[...])
    even, odd = inner[:tile], inner[tile:]

    edge = jnp.zeros((tile, lane), jnp.float32)
    even = jnp.concatenate([edge, even, jnp.zeros((tile, tile), jnp.float32)], axis=1)
    part_right.wait()
    from_left = got_left[0].astype(jnp.float32)
    out[0] = even + jnp.concatenate([from_left, jnp.zeros((tile, 3 * tile), jnp.float32)], axis=1)
    part_left.wait()
    from_right = got_right[0].astype(jnp.float32)
    odd = jnp.concatenate([odd, edge], axis=1) + jnp.concatenate([edge, from_right], axis=1)
    out[1] = jnp.concatenate([jnp.zeros((tile, tile), jnp.float32), odd], axis=1)

    swap_half.wait_send()

    @pl.when(is_inner)
    def _():
        half_low.wait_send()
        half_high.wait_send()

    @pl.when(is_outer)
    def _():
        to_right.wait_send()
        to_left.wait_send()


def shards(a_tiles, p_tiles, acols, agg):
    rows_dev, tile, width = a_tiles.shape
    links = width // tile
    grp = lax.axis_size("grp")
    ring = lax.axis_size("rows") * grp
    halo = REACH
    bf16, f32 = jnp.bfloat16, jnp.float32
    pairs = (links + 1) // 2
    lane = 2 * tile
    n_all = rows_dev + 2 * halo
    return pl.pallas_call(
        functools.partial(galerkin_kernel, rows_dev, tile, links, ring, grp),
        out_shape=jax.ShapeDtypeStruct((rows_dev // RATIO, tile, 11 * tile), f32),
        in_specs=[
            pl.BlockSpec(memory_space=pltpu.SMEM),
            pl.BlockSpec(memory_space=pltpu.VMEM),
            pl.BlockSpec(memory_space=pl.ANY),
            pl.BlockSpec(memory_space=pl.ANY),
        ],
        out_specs=pl.BlockSpec(memory_space=pltpu.VMEM),
        scratch_shapes=[
            pltpu.VMEM((rows_dev, lane), jnp.int32),
            pltpu.SMEM((rows_dev, lane), jnp.int32),
            pltpu.VMEM((2 * pairs, rows_dev, tile, lane), bf16),
            pltpu.VMEM((rows_dev, tile, tile), bf16),
            pltpu.VMEM((rows_dev, tile, 3 * tile), bf16),
            pltpu.VMEM((rows_dev, 3 * tile // 2, lane), bf16),
            pltpu.VMEM((2, rows_dev, 3 * tile // 2, lane), bf16),
            pltpu.VMEM((rows_dev * tile, n_all * tile), bf16),
            pltpu.VMEM((n_all * tile, 4 * tile), bf16),
            pltpu.VMEM((4 * tile, rows_dev * tile), bf16),
            pltpu.VMEM((rows_dev * tile, 8 * tile), bf16),
            pltpu.VMEM((rows_dev * tile, 4 * tile), f32),
            pltpu.VMEM((2, tile, 8 * tile), bf16),
            pltpu.VMEM((2, tile, 8 * tile), bf16),
            pltpu.SemaphoreType.DMA((pairs,)),
            pltpu.SemaphoreType.DMA,
            pltpu.SemaphoreType.DMA,
            pltpu.SemaphoreType.DMA((3,)),
            pltpu.SemaphoreType.DMA((3,)),
            pltpu.SemaphoreType.DMA((2,)),
            pltpu.SemaphoreType.DMA((2,)),
        ],
        compiler_params=pltpu.CompilerParams(
            collective_id=0, has_side_effects=True, vmem_limit_bytes=58 * 2**20
        ),
    )(agg, acols, a_tiles, p_tiles)


def solution(mesh):
    return jax.shard_map(
        shards,
        mesh=mesh,
        in_specs=(
            P(("rows", "grp"), None, None),
            P(("rows", "grp"), None, None),
            P(("rows", "grp"), None),
            P(),
        ),
        out_specs=P(("rows", "grp"), None, None),
        check_vma=False,
    )
```

```python
import functools

import jax
import jax.numpy as jnp
from jax import lax
from jax.experimental import pallas as pl
from jax.experimental.pallas import tpu as pltpu
from jax.sharding import PartitionSpec as P

RATIO = 8
REACH = 14
MESH = pl.DeviceIdType.MESH


def dot(a, b):
    return jnp.dot(a, b, preferred_element_type=jnp.float32)


def galerkin_kernel(
    rows_dev, tile, links, ring, grp, agg, acols, a_hbm, p_hbm, out,
    found, tbl, a2, a_tail, p_own, packed, near, ad, p4, p4t, band, part, got_left, got_right,
    a_sem, p_sem, t_sem, halo_send, halo_recv, part_send, part_recv,
):
    lane = 2 * tile
    halo = REACH
    pairs = (links + 1) // 2
    groups = rows_dev // 2 + halo
    me = lax.axis_index("rows") * grp + lax.axis_index("grp")
    right, left = lax.rem(me + 1, ring), lax.rem(me + ring - 1, ring)

    def device(d):
        return (d // grp, lax.rem(d, grp))

    full = links // 2
    a_copies = [
        pltpu.make_async_copy(
            a_hbm.at[:, :, pl.ds(g * lane, lane)], a2.at[g], a_sem.at[g]
        )
        for g in range(full)
    ]
    a_copies.append(
        pltpu.make_async_copy(
            a_hbm.at[:, :, pl.ds(full * lane, tile)], a_tail, a_sem.at[full]
        )
    )
    p_copy = pltpu.make_async_copy(p_hbm, p_own, p_sem)
    p_copy.start()
    for copy in a_copies:
        copy.start()

    barrier = pltpu.get_barrier_semaphore()
    spot4 = lax.rem(me, 4)
    core = spot4 // 2
    mate = lax.rem(me + 2 + ring - 4 * core, ring)
    for partner in (left, right, mate):
        pl.semaphore_signal(barrier, inc=1, device_id=device(partner), device_id_type=MESH)

    p_copy.wait()
    for r in range(rows_dev):
        x = p_own[r]
        packed[r, :tile] = x[:, :lane]
        packed[r, tile:] = jnp.concatenate([x[: tile // 2, lane:], x[tile // 2 :, lane:]], axis=1)
    pl.semaphore_wait(barrier, 3)

    is_inner = (spot4 == 1) | (spot4 == 2)
    mid, spare = rows_dev // 2, rows_dev - halo

    def send(src, side, start, count, sem, arrival, target):
        return pltpu.make_async_remote_copy(
            src.at[pl.ds(start, count)], near.at[side, pl.ds(start, count)],
            halo_send.at[sem], halo_recv.at[arrival],
            device_id=device(target), device_id_type=MESH,
        )

    to_right = send(packed, 0, spare, halo, 0, 2, right)
    to_left = send(packed, 1, 0, halo, 1, 2, left)
    half_low = send(packed, 1, 0, mid, 0, 0, left)
    half_high = send(packed, 0, mid, mid, 1, 0, right)
    got_half = near.at[1 - core]
    swap_half = send(got_half, core, mid * core, mid, 2, 1, mate)
    in_half = send(packed, 1 - core, mid * core, mid, 2, 0, mate)
    in_swap = send(packed, 1 - core, mid * (1 - core), mid, 2, 1, mate)
    in_full = send(packed, core, spare * (1 - core), halo, 2, 2, mate)

    @pl.when(is_inner)
    def _():
        half_low.start()
        half_high.start()

    @pl.when(spot4 == 0)
    def _():
        to_left.start()
        to_right.start()

    @pl.when(spot4 == 3)
    def _():
        to_right.start()
        to_left.start()

    total_rows = rows_dev * ring
    first_row = me * rows_dev
    row = lax.broadcasted_iota(jnp.int32, found.shape, 0)
    spot = lax.broadcasted_iota(jnp.int32, found.shape, 1)
    half = spot & 1
    table = (half if links % 2 == 0 else 1 - half) * pairs + links // 2
    for k in range(links):
        at = jnp.broadcast_to(acols[:, k : k + 1], found.shape) - first_row - row + REACH
        at = jnp.where(at < 0, at + total_rows, at)
        at = jnp.where(at >= total_rows, at - total_rows, at) + (row & 1)
        side = half if k % 2 == 0 else 1 - half
        table = jnp.where(at == spot, side * pairs + k // 2, table)
    found[...] = table
    t_copy = pltpu.make_async_copy(found, tbl, t_sem)
    t_copy.start()

    low_half = lax.broadcasted_iota(jnp.int32, (tile, lane), 1) < tile

    def place(p_ref, from_row, count, base):
        nothing = jnp.zeros((tile, lane), jnp.bfloat16)
        for r in range(count):
            x, y = p_ref[from_row + r, :tile], p_ref[from_row + r, tile:]
            turned = pltpu.roll(y, tile, 1)
            rest_low = jnp.concatenate([y, turned], axis=0)
            rest_high = jnp.concatenate([turned, y], axis=0)
            x_turned = pltpu.roll(x, tile, 1)
            own = agg[lax.rem(first_row + total_rows - halo + base + r, total_rows)] & 1
            odd = jnp.full((tile, lane), own, jnp.int32).astype(jnp.float32).astype(jnp.bfloat16)
            even = jnp.bfloat16(1) - odd
            rows = slice((base + r) * tile, (base + r + 1) * tile)
            p4[rows, :lane] = x * even + jnp.where(low_half, nothing, x_turned) * odd
            p4[rows, lane:] = (
                jnp.where(low_half, rest_low, nothing) * even
                + jnp.where(low_half, x_turned, rest_high) * odd
            )

    place(packed, 0, rows_dev, halo)
    p4t[...] = p4[halo * tile : (halo + rows_dev) * tile, :].T

    for copy in a_copies:
        copy.wait()
    gap = jnp.zeros((tile, tile), jnp.bfloat16)
    for r in range(rows_dev):
        x = a_tail[r]
        a2[full, r] = jnp.concatenate([x, gap], axis=1)
        a2[pairs + full, r] = jnp.concatenate([gap, x], axis=1)

    def swap(g, carry):
        for r in range(rows_dev):
            a2[pairs + g, r] = pltpu.roll(a2[g, r], tile, 1)
        return carry

    lax.fori_loop(0, full, swap, 0)
    t_copy.wait()

    span = REACH + 1
    first_half = lax.broadcasted_iota(jnp.int32, (tile, lane), 1) < tile

    def gather(r2, carry):
        for parity in range(2):
            r = 2 * r2 + parity
            rows = pl.ds(pl.multiple_of(r * tile, tile), tile)
            for g in range(span):
                x0 = a2[tbl[r, 2 * g], r]
                x1 = a2[tbl[r, 2 * g + 1], r]
                ad[rows, pl.ds(pl.multiple_of((r2 + g) * lane, lane), lane)] = jnp.where(
                    first_half, x0, x1
                )
        return carry

    lax.fori_loop(0, rows_dev // 2, gather, 0)

    empty = jnp.zeros((2 * tile, lane), jnp.bfloat16)
    for r2 in range(rows_dev // 2):
        for g in range(groups):
            if g < r2 or g >= r2 + span:
                ad[r2 * lane : (r2 + 1) * lane, g * lane : (g + 1) * lane] = empty

    chunk = 4 * tile
    k_left, k_own, k_all = halo * tile, (halo + rows_dev) * tile, (2 * halo + rows_dev) * tile
    own_sum = part

    def own_part(c, carry):
        rows = pl.ds(pl.multiple_of(c * chunk, chunk), chunk)
        own_sum[rows, :] = dot(ad[rows, k_left:k_own], p4[k_left:k_own, :])
        return carry

    lax.fori_loop(0, rows_dev // 4, own_part, 0)

    in_half.wait_recv()
    swap_half.start()
    in_full.wait_recv()
    in_swap.wait_recv()
    place(near.at[0], spare, halo, 0)
    place(near.at[1], 0, halo, halo + rows_dev)

    def ends(c, carry):
        rows = pl.ds(pl.multiple_of(c * chunk, chunk), chunk)
        low = dot(ad[rows, 0:k_left], p4[0:k_left, :])
        high = dot(ad[rows, k_own:k_all], p4[k_own:k_all, :])
        mid = own_sum[rows, :]
        band[rows, 0:lane] = low[:, :lane].astype(jnp.bfloat16)
        band[rows, lane : 2 * lane] = (low[:, lane:] + mid[:, :lane]).astype(jnp.bfloat16)
        band[rows, 2 * lane : 3 * lane] = (high[:, :lane] + mid[:, lane:]).astype(jnp.bfloat16)
        band[rows, 3 * lane : 4 * lane] = high[:, lane:].astype(jnp.bfloat16)
        return carry

    lax.fori_loop(0, rows_dev // 4, ends, 0)

    send_left, send_right = got_left.at[1], got_right.at[1]
    outer = dot(p4t[0:tile, :], band[...])
    send_left[...] = outer.astype(jnp.bfloat16)
    part_left = pltpu.make_async_remote_copy(
        send_left, got_right.at[0],
        part_send.at[0], part_recv.at[0], device_id=device(left), device_id_type=MESH,
    )
    part_left.start()
    outer = dot(p4t[3 * tile : 4 * tile, :], band[...])
    send_right[...] = outer.astype(jnp.bfloat16)
    part_right = pltpu.make_async_remote_copy(
        send_right, got_left.at[0],
        part_send.at[1], part_recv.at[1], device_id=device(right), device_id_type=MESH,
    )
    part_right.start()
    inner = dot(p4t[tile : 3 * tile, :], band[...])
    even, odd = inner[:tile], inner[tile:]

    edge = jnp.zeros((tile, lane), jnp.float32)
    even = jnp.concatenate([edge, even, jnp.zeros((tile, tile), jnp.float32)], axis=1)
    part_right.wait()
    from_left = got_left[0].astype(jnp.float32)
    out[0] = even + jnp.concatenate([from_left, jnp.zeros((tile, 3 * tile), jnp.float32)], axis=1)
    part_left.wait()
    from_right = got_right[0].astype(jnp.float32)
    odd = jnp.concatenate([odd, edge], axis=1) + jnp.concatenate([edge, from_right], axis=1)
    out[1] = jnp.concatenate([jnp.zeros((tile, tile), jnp.float32), odd], axis=1)

    swap_half.wait_send()

    @pl.when(is_inner)
    def _():
        half_low.wait_send()
        half_high.wait_send()

    @pl.when((spot4 == 0) | (spot4 == 3))
    def _():
        to_right.wait_send()
        to_left.wait_send()


def shards(a_tiles, p_tiles, acols, agg):
    rows_dev, tile, width = a_tiles.shape
    links = width // tile
    grp = lax.axis_size("grp")
    ring = lax.axis_size("rows") * grp
    halo = REACH
    bf16, f32 = jnp.bfloat16, jnp.float32
    pairs = (links + 1) // 2
    lane = 2 * tile
    n_all = rows_dev + 2 * halo
    return pl.pallas_call(
        functools.partial(galerkin_kernel, rows_dev, tile, links, ring, grp),
        out_shape=jax.ShapeDtypeStruct((rows_dev // RATIO, tile, 11 * tile), f32),
        in_specs=[
            pl.BlockSpec(memory_space=pltpu.SMEM),
            pl.BlockSpec(memory_space=pltpu.VMEM),
            pl.BlockSpec(memory_space=pl.ANY),
            pl.BlockSpec(memory_space=pl.ANY),
        ],
        out_specs=pl.BlockSpec(memory_space=pltpu.VMEM),
        scratch_shapes=[
            pltpu.VMEM((rows_dev, lane), jnp.int32),
            pltpu.SMEM((rows_dev, lane), jnp.int32),
            pltpu.VMEM((2 * pairs, rows_dev, tile, lane), bf16),
            pltpu.VMEM((rows_dev, tile, tile), bf16),
            pltpu.VMEM((rows_dev, tile, 3 * tile), bf16),
            pltpu.VMEM((rows_dev, 3 * tile // 2, lane), bf16),
            pltpu.VMEM((2, rows_dev, 3 * tile // 2, lane), bf16),
            pltpu.VMEM((rows_dev * tile, n_all * tile), bf16),
            pltpu.VMEM((n_all * tile, 4 * tile), bf16),
            pltpu.VMEM((4 * tile, rows_dev * tile), bf16),
            pltpu.VMEM((rows_dev * tile, 8 * tile), bf16),
            pltpu.VMEM((rows_dev * tile, 4 * tile), f32),
            pltpu.VMEM((2, tile, 8 * tile), bf16),
            pltpu.VMEM((2, tile, 8 * tile), bf16),
            pltpu.SemaphoreType.DMA((pairs,)),
            pltpu.SemaphoreType.DMA,
            pltpu.SemaphoreType.DMA,
            pltpu.SemaphoreType.DMA((3,)),
            pltpu.SemaphoreType.DMA((3,)),
            pltpu.SemaphoreType.DMA((2,)),
            pltpu.SemaphoreType.DMA((2,)),
        ],
        compiler_params=pltpu.CompilerParams(
            collective_id=0, has_side_effects=True, vmem_limit_bytes=52 * 2**20
        ),
    )(agg, acols, a_tiles, p_tiles)


def solution(mesh):
    return jax.shard_map(
        shards,
        mesh=mesh,
        in_specs=(
            P(("rows", "grp"), None, None),
            P(("rows", "grp"), None, None),
            P(("rows", "grp"), None),
            P(),
        ),
        out_specs=P(("rows", "grp"), None, None),
        check_vma=False,
    )
```
